32 devices in a mesh: gx: 4 (over y, core), gy: 4 (over z), gz: 2 (over x).
Axes of the slice: x: 2, y: 2, z: 4, core: 2. Of those that a mesh axis runs over, the one named last changes fastest.
Arguments:
- fine_disp: float32 [3, 8, 128, 2048], P(None, None, ('gy', 'gz'), 'gx'), may hold values from -6 to 6
- fine_prev: float32 [3, 8, 128, 2048], P(None, None, ('gy', 'gz'), 'gx'), may hold values from -6 to 6
- fine_media: float32 [4, 8, 128, 2048], P(None, None, ('gy', 'gz'), 'gx'), may hold values from 0.5 to 2
- coarse_disp: float32 [3, 8, 64, 1024], P(None, None, 'gy', ('gx', 'gz')), may hold values from -6 to 6
- coarse_prev: float32 [3, 8, 64, 1024], P(None, None, 'gy', ('gx', 'gz')), may hold values from -6 to 6
- coarse_media: float32 [3, 8, 64, 1024], P(None, None, 'gy', ('gx', 'gz')), may hold values from 0.5 to 2
- source_cell: int32 [4, 8, 8192], P('gx', ('gy', 'gz')), may hold values from 0 to 8191, as said below
- target_cell: int32 [4, 8, 8192], P('gx', ('gy', 'gz')), may hold values from 0 to 2047, as said below
- target_owner: int32 [4, 8, 8192], P('gx', ('gy', 'gz')), may hold values from 0 to 7, as said below
- target_weight: float32 [4, 8, 8192], P('gx', ('gy', 'gz')), may hold values from 0.1 to 0.4
- used_count: int32 [4, 8], P('gx', ('gy', 'gz')), may hold values from 4096 to 8192, as said below
Outputs:
- fine_next: float32 [3, 8, 128, 2048], P(None, None, ('gy', 'gz'), 'gx')
- coarse_next: float32 [3, 8, 64, 1024], P(None, None, 'gy', ('gx', 'gz'))
- ghost_plane: float32 [3, 64, 1024], P(None, 'gy', ('gx', 'gz'))
The draws below stay inside these ranges and needn't reach their ends.
Inputs may be any that keep to these rules, and one draw needn't show every extreme that they name: `source_cell`: each block lists every cell of its bottom plane once, as y * 512 + x in the block, in an order drawn from the seed. `target_cell`: row * 128 + column in the owner's block of the ghost plane. `target_owner`: the owner has the same gy index as the device that holds the entry. `used_count`: entries at and past the count are padding.
All inputs are finite; a program needn't handle non-finite values.
Results may differ from the reference program's by a relative error of at most 0.000075.
Values sent between devices are 32-bit elements; how exact they have to be, the bound alone decides.
A program may use at most 64 MiB of HBM per device.

```python
import math
import jax
import jax.numpy as jnp
from jax import lax

CX = 512
CY = 16
KF = 8
KC = 8
BX = 4
BY = 8
NXF = 2048
NYF = 128
CXC = 128
CYC = 16
NXC = 1024
NYC = 64
R = 8192
N_GZ = 2


def interface_layout(key):
    keys = jax.random.split(jax.random.fold_in(key, 11), BX * BY)
    orders = jax.vmap(lambda single: jax.random.permutation(single, R))(keys)
    orders = orders.reshape(BX, BY, R).astype(jnp.int32)
    block_y = jnp.arange(BY, dtype=jnp.int32)[None, :, None]
    peer_pick = jax.random.randint(jax.random.fold_in(key, 13), (BX, BY, R), 0, N_GZ).astype(jnp.int32)
    owners = block_y // N_GZ * N_GZ + peer_pick
    targets = jax.random.randint(jax.random.fold_in(key, 17), (BX, BY, R), 0, CXC * CYC).astype(jnp.int32)
    return (orders, targets.astype(jnp.int32), owners.astype(jnp.int32))


def draw_source_cell(key, part):
    return interface_layout(key)[0]


def draw_target_cell(key, part):
    return interface_layout(key)[1]


def draw_target_owner(key, part):
    return interface_layout(key)[2]


def draw_used_count(key, part):
    total = BX * BY
    counts = jax.random.randint(jax.random.fold_in(key, 29), (total,), R // 2, R + 1)
    first_pick = jax.random.randint(jax.random.fold_in(key, 31), (), 0, total)
    offset = jax.random.randint(jax.random.fold_in(key, 37), (), 0, total - 1)
    second_pick = (first_pick + 1 + offset) % total
    places = jnp.arange(total, dtype=jnp.int32)
    counts = jnp.where(places == first_pick, R, counts)
    counts = jnp.where(places == second_pick, R // 2, counts)
    return counts.reshape(BX, BY).astype(jnp.int32)


def levels(key, dims, cuts, low, high):
    def one(dim, shards_of):
        steps = jax.random.uniform(jax.random.fold_in(jax.random.fold_in(key, 6), dim), (shards_of,), jnp.float32, low / len(cuts), high / len(cuts))
        return jnp.repeat(jnp.exp(steps), dims[dim] // shards_of).reshape((-1,) + (1,) * (len(dims) - dim - 1))

    level = one(*cuts[0])
    for cut in cuts[1:]:
        level = level * one(*cut)
    return level


def gaussian(own_key, shape, spread, reach, pieces=(), kind=jnp.bfloat16):
    entries = jax.random.normal(own_key, shape, jnp.float32) * spread
    if len(pieces) > 0:
        entries = levels(own_key, shape, pieces, -0.22, 0.18) * entries
    return jnp.clip(entries, min=-reach, max=reach).astype(kind)


def setup_inputs(seed: int = 0) -> dict:
    seeds = jax.random.split(jax.random.key(seed), 12)
    return {
        "fine_disp": gaussian(seeds[0], (3, KF, NYF, NXF), 1.0, 6.0, ((2, 8), (3, 4)), jnp.float32),
        "fine_prev": gaussian(seeds[1], (3, KF, NYF, NXF), 1.0, 6.0, ((2, 8), (3, 4)), jnp.float32),
        "fine_media": jnp.clip(jnp.exp(math.log(2.0) - 1.3862944 * jax.random.uniform(seeds[2], (4, KF, NYF, NXF), jnp.float32) ** levels(seeds[2], (4, KF, NYF, NXF), ((2, 8), (3, 4)), -0.2, 0.2)), 0.5, 2.0),
        "coarse_disp": gaussian(seeds[3], (3, KC, NYC, NXC), 1.0, 6.0, ((2, 4), (3, 8)), jnp.float32),
        "coarse_prev": gaussian(seeds[4], (3, KC, NYC, NXC), 1.0, 6.0, ((2, 4), (3, 8)), jnp.float32),
        "coarse_media": jnp.clip(jnp.exp(math.log(2.0) - 1.3862944 * jax.random.uniform(seeds[5], (3, KC, NYC, NXC), jnp.float32) ** levels(seeds[5], (3, KC, NYC, NXC), ((2, 4), (3, 8)), -0.2, 0.2)), 0.5, 2.0),
        "source_cell": draw_source_cell(jax.random.fold_in(seeds[11], 71), 0),
        "target_cell": draw_target_cell(jax.random.fold_in(seeds[11], 71), 0),
        "target_owner": draw_target_owner(jax.random.fold_in(seeds[11], 71), 0),
        "target_weight": jnp.clip(0.1 + 0.3 * jax.random.uniform(seeds[9], (BX, BY, R), jnp.float32) ** levels(seeds[9], (BX, BY, R), ((0, 4), (1, 8)), -0.2, 0.2), 0.1, 0.4),
        "used_count": draw_used_count(jax.random.fold_in(seeds[11], 71), 0),
    }


step_scale = 0.02


def stencil(padded, axis):
    count = padded.shape[axis] - 4
    parts = [lax.slice_in_dim(padded, shift, shift + count, axis=axis) for shift in range(5)]
    return (-parts[0] + 16.0 * parts[1] - 30.0 * parts[2] + 16.0 * parts[3] - parts[4]) / 12.0


def pad_along(field, axis):
    widths = [(0, 0)] * field.ndim
    widths[axis] = (2, 2)
    return jnp.pad(field, widths)


def accelerate(media_shear, media_first, density, second_x, second_y, vertical):
    laplace = second_x + second_y + vertical
    along = jnp.stack([second_x[0], second_y[1], vertical[2]])
    return (media_shear * laplace + (media_first + media_shear) * along) / density


def reference(fine_disp, fine_prev, fine_media, coarse_disp, coarse_prev, coarse_media, source_cell, target_cell, target_owner, target_weight, used_count):
    block_x = jnp.arange(BX, dtype=jnp.int32)[:, None, None]
    block_y = jnp.arange(BY, dtype=jnp.int32)[None, :, None]
    fine_y = block_y * CY + source_cell // CX
    fine_x = block_x * CX + source_cell % CX
    bottom = fine_disp[:, KF - 1]
    values = bottom[:, fine_y, fine_x]
    usable = (jnp.arange(R, dtype=jnp.int32)[None, None, :] < used_count[:, :, None]).astype(jnp.float32)
    scaled = target_weight * usable
    ghost_y = (target_owner // N_GZ) * CYC + target_cell // CXC
    ghost_x = (block_x * N_GZ + target_owner % N_GZ) * CXC + target_cell % CXC
    target_flat = (ghost_y * NXC + ghost_x).reshape(-1)
    contrib = (values * scaled[None]).reshape(3, -1)
    ghost_plane = jnp.zeros((3, NYC * NXC), jnp.float32).at[:, target_flat].add(contrib).reshape(3, NYC, NXC)

    second_x = stencil(pad_along(fine_disp, 3), 3)
    second_y = stencil(pad_along(fine_disp, 2), 2)
    second_z = stencil(pad_along(fine_disp, 1), 1)
    vertical = fine_media[3] * second_z
    accel = accelerate(fine_media[0], fine_media[1], fine_media[2], second_x, second_y, vertical)
    fine_next = 2.0 * fine_disp - fine_prev + step_scale * accel

    upper = jnp.concatenate([jnp.zeros((3, 1, NYC, NXC), jnp.float32), ghost_plane[:, None], coarse_disp, jnp.zeros((3, 2, NYC, NXC), jnp.float32)], axis=1)
    coarse_x = stencil(pad_along(coarse_disp, 3), 3)
    coarse_y = stencil(pad_along(coarse_disp, 2), 2)
    coarse_z = stencil(upper, 1)
    accel_c = accelerate(coarse_media[0], coarse_media[1], coarse_media[2], coarse_x, coarse_y, coarse_z) / 4.0
    coarse_next = 2.0 * coarse_disp - coarse_prev + step_scale * accel_c
    return fine_next, coarse_next, ghost_plane
```

```python
import functools

import jax
import jax.numpy as jnp
from jax import lax
from jax.experimental import pallas as pl
from jax.experimental.pallas import tpu as pltpu
from jax.sharding import PartitionSpec as P

step_scale = 0.02
MESH = pl.DeviceIdType.MESH
CHUNK_ROWS = 4


def rows_of(ref, start, count):
    return jnp.concatenate([ref[pl.ds(start + q, 1), :] for q in range(count)], axis=1)


def second(values):
    low2, low1, mid, high1, high2 = values
    return (16.0 * (low1 + high1) - (low2 + high2) - 30.0 * mid) * (1.0 / 12.0)


def pack_columns(ref, out_ref, first, lane0, depth, comps):
    rows = out_ref.shape[0]
    lane = lax.broadcasted_iota(jnp.int32, (rows, 128), 1) // 2
    total = jnp.zeros((rows, 128), jnp.float32)
    for c in range(comps):
        for z in range(depth):
            k = c * depth + z
            tile = ref[c, 2 + z, 8 : 8 + rows, first : first + 128]
            total = jnp.where(lane == k, pltpu.roll(tile, (2 * k - lane0) % 128, 1), total)
    out_ref[...] = total


def stencil_xy(ref, from_low, from_high, c, z, k):
    rows = from_low.shape[0]
    cols = ref.shape[3]
    wide = cols + 256
    mid = ref[c, 2 + z, 8 : 8 + rows, :]
    left = pltpu.roll(from_low[...], 126 - 2 * k, 1)
    right = pltpu.roll(from_high[...], (128 - 2 * k) % 128, 1)
    ext = jnp.concatenate([left, mid, right], axis=1)
    moved = [pltpu.roll(ext, s % wide, 1)[:, 128 : 128 + cols] for s in (2, 1, -1, -2)]
    along_x = second((moved[0], moved[1], mid, moved[2], moved[3]))
    shifted = [ref[c, 2 + z, 6 + s : 6 + s + rows, :] for s in (0, 1, 3, 4)]
    along_y = second((shifted[0], shifted[1], mid, shifted[2], shifted[3]))
    along_z = second(
        (
            ref[c, z, 8 : 8 + rows, :],
            ref[c, z + 1, 8 : 8 + rows, :],
            mid,
            ref[c, z + 3, 8 : 8 + rows, :],
            ref[c, z + 4, 8 : 8 + rows, :],
        )
    )
    return mid, along_x, along_y, along_z


def kernel(
    sizes,
    count_ref,
    fine_hbm,
    fprev_hbm,
    fmedia_hbm,
    coarse_hbm,
    cprev_hbm,
    cmedia_hbm,
    source_hbm,
    target_hbm,
    owner_hbm,
    weight_hbm,
    fnext_hbm,
    cnext_hbm,
    ghost_hbm,
    fp,
    fprev,
    fmedia,
    cp,
    cprev,
    cmedia,
    source,
    target,
    owner,
    weight,
    fnext,
    cnext,
    ghost,
    fy_out,
    fy_in,
    fx_out,
    fx_in,
    cy_out,
    cy_in,
    cx_out,
    cx_in,
    src_lo,
    src_hi,
    tgt_lo,
    tgt_hi,
    total,
    partial,
    peer_part,
    load_sem,
    store_sem,
    send_sem,
    recv_sem,
):
    n_gx, n_gy, n_gz = sizes
    comps, depth, rows, cols = fprev.shape
    crows, ccols = cprev.shape[2:]
    gx = lax.axis_index("gx")
    gy = lax.axis_index("gy")
    gz = lax.axis_index("gz")

    loads = [
        (fine_hbm, fp.at[:, 2 : 2 + depth, 8 : 8 + rows, :]),
        (source_hbm, source),
        (target_hbm, target),
        (owner_hbm, owner),
        (weight_hbm, weight),
        (coarse_hbm, cp.at[:, 2 : 2 + depth, 8 : 8 + crows, :]),
        (fmedia_hbm, fmedia),
        (fprev_hbm, fprev),
        (cmedia_hbm, cmedia),
        (cprev_hbm, cprev),
    ]
    load = [pltpu.make_async_copy(a, b, load_sem.at[i]) for i, (a, b) in enumerate(loads)]
    for copy in load:
        copy.start()

    fine_y = gy * n_gz + gz
    coarse_x = gx * n_gz + gz
    has = [
        fine_y > 0,
        fine_y < n_gy * n_gz - 1,
        gx > 0,
        gx < n_gx - 1,
        gy > 0,
        gy < n_gy - 1,
        coarse_x > 0,
        coarse_x < n_gx * n_gz - 1,
    ]
    y_low, y_high = fine_y - 1, fine_y + 1
    x_low, x_high = coarse_x - 1, coarse_x + 1
    where_to = [
        (gx, lax.div(y_low, n_gz), lax.rem(y_low, n_gz)),
        (gx, lax.div(y_high, n_gz), lax.rem(y_high, n_gz)),
        (gx - 1, gy, gz),
        (gx + 1, gy, gz),
        (gx, gy - 1, gz),
        (gx, gy + 1, gz),
        (lax.div(x_low, n_gz), gy, lax.rem(x_low, n_gz)),
        (lax.div(x_high, n_gz), gy, lax.rem(x_high, n_gz)),
    ]
    buffers = [fy_out, fy_out, fx_out, fx_out, cy_out, cy_out, cx_out, cx_out]
    landing = [fy_in, fy_in, fx_in, fx_in, cy_in, cy_in, cx_in, cx_in]
    peer = (gx, gy, n_gz - 1 - gz)

    barrier = pltpu.get_barrier_semaphore()
    expected = 1
    pl.semaphore_signal(barrier, inc=1, device_id=peer, device_id_type=MESH)
    for n in range(8):
        expected = expected + has[n].astype(jnp.int32)

        @pl.when(has[n])
        def _():
            pl.semaphore_signal(barrier, inc=1, device_id=where_to[n], device_id_type=MESH)

        @pl.when(jnp.logical_not(has[n]))
        def _():
            landing[n][n % 2] = jnp.zeros(landing[n].shape[1:], jnp.float32)

    zero_fine = jnp.zeros((comps, 2, rows, cols), jnp.float32)
    fp[:, 0:2, 8 : 8 + rows, :] = zero_fine
    fp[:, 2 + depth : 4 + depth, 8 : 8 + rows, :] = zero_fine
    zero_coarse = jnp.zeros((comps, 2, crows, ccols), jnp.float32)
    cp[:, 0:2, 8 : 8 + crows, :] = zero_coarse
    cp[:, 2 + depth : 4 + depth, 8 : 8 + crows, :] = zero_coarse

    def halo(n):
        return pltpu.make_async_remote_copy(
            src_ref=buffers[n].at[n % 2],
            dst_ref=landing[n].at[1 - n % 2],
            send_sem=send_sem.at[n],
            recv_sem=recv_sem.at[n],
            device_id=where_to[n],
            device_id_type=MESH,
        )

    load[0].wait()
    for side, first in ((0, 8), (1, 8 + rows - 2)):
        fy_out[side] = fp[:, 2 : 2 + depth, first : first + 2, :]
    pack_columns(fp, fx_out.at[0], 0, 0, depth, comps)
    pack_columns(fp, fx_out.at[1], cols - 128, 126, depth, comps)
    pl.semaphore_wait(barrier, expected)
    for n in range(4):

        @pl.when(has[n])
        def _():
            halo(n).start()

    load[5].wait()
    for side, first in ((0, 8), (1, 8 + crows - 2)):
        cy_out[side] = cp[:, 2 : 2 + depth, first : first + 2, :]
    pack_columns(cp, cx_out.at[0], 0, 0, depth, comps)
    pack_columns(cp, cx_out.at[1], ccols - 128, 126, depth, comps)
    for n in range(4, 8):

        @pl.when(has[n])
        def _():
            halo(n).start()

    half = 256
    halves = cols // half
    pieces = []
    for c in range(comps):
        for h in range(halves):
            pieces.append(fp[c, 1 + depth, 8 : 8 + rows, h * half : (h + 1) * half])
    plane = jnp.concatenate(pieces, axis=0)
    plane_high = plane.astype(jnp.bfloat16)
    plane_low = (plane - plane_high.astype(jnp.float32)).astype(jnp.bfloat16)
    plane = jnp.concatenate([plane_high, plane_low], axis=0)
    group = halves * rows

    for i in range(1, 5):
        load[i].wait()
    cell = source[...]
    src_lo[...] = (cell % half).astype(jnp.float32)
    src_hi[...] = ((cell % cols) // half * rows + cell // cols).astype(jnp.float32)
    cell = target[...]
    tgt_lo[...] = (cell % ccols).astype(jnp.float32)
    tgt_hi[...] = (owner[...] % n_gz * crows + cell // ccols).astype(jnp.float32)
    entry_rows = source.shape[0]
    place = lax.broadcasted_iota(jnp.int32, (entry_rows, 128), 0) * 128
    place = place + lax.broadcasted_iota(jnp.int32, (entry_rows, 128), 1)
    weight[...] = jnp.where(place < count_ref[0, 0], weight[...], 0.0)

    wide = CHUNK_ROWS * 128
    base = lax.broadcasted_iota(jnp.int32, (16, wide), 0).astype(jnp.float32).astype(jnp.bfloat16)
    group_base = lax.broadcasted_iota(jnp.int32, (group, wide), 0).astype(jnp.float32)
    one = jnp.ones((16, wide), jnp.bfloat16)
    zero = jnp.zeros((16, wide), jnp.bfloat16)
    total[...] = jnp.zeros_like(total)

    def spread(row):
        return jnp.broadcast_to(row, (16, wide)).astype(jnp.bfloat16)

    def onehot(ref, start, count):
        index = spread(rows_of(ref, start, CHUNK_ROWS))
        return jnp.concatenate(
            [jnp.where(index == base + float(16 * t), one, zero) for t in range(count // 16)],
            axis=0,
        )

    @pl.loop(0, entry_rows // CHUNK_ROWS)
    def _(turn):
        start = turn * CHUNK_ROWS
        picked = jnp.dot(plane, onehot(src_lo, start, half), preferred_element_type=jnp.float32)
        picked = picked[: comps * group] + picked[comps * group :]
        row_mask = jnp.broadcast_to(rows_of(src_hi, start, CHUNK_ROWS), (group, wide)) == group_base
        scale = rows_of(weight, start, CHUNK_ROWS)
        target_row = spread(rows_of(tgt_hi, start, CHUNK_ROWS))
        masks = [target_row == base + float(16 * t) for t in range(n_gz * crows // 16)]
        high_part, low_part = [], []
        for c in range(comps):
            value = jnp.where(row_mask, picked[c * group : (c + 1) * group], 0.0)
            value = jnp.sum(value, axis=0, keepdims=True) * scale
            value = jnp.broadcast_to(value, (16, wide))
            high = value.astype(jnp.bfloat16)
            low = (value - high.astype(jnp.float32)).astype(jnp.bfloat16)
            high_part += [jnp.where(mask, high, zero) for mask in masks]
            low_part += [jnp.where(mask, low, zero) for mask in masks]
        total[...] += lax.dot_general(
            jnp.concatenate(high_part + low_part, axis=0),
            onehot(tgt_lo, start, ccols),
            (((1,), (1,)), ((), ())),
            preferred_element_type=jnp.float32,
        )

    span = n_gz * crows
    for c in range(comps):
        partial[c] = (
            total[c * span : (c + 1) * span, :] + total[(comps + c) * span : (comps + c + 1) * span, :]
        )
    swap = pltpu.make_async_remote_copy(
        src_ref=partial.at[:, pl.ds(pl.multiple_of((n_gz - 1 - gz) * crows, 8), crows), :],
        dst_ref=peer_part,
        send_sem=send_sem.at[8],
        recv_sem=recv_sem.at[8],
        device_id=peer,
        device_id_type=MESH,
    )
    swap.start()

    def arrive(n):
        @pl.when(has[n ^ 1])
        def _():
            halo(n).wait_recv()

    for n in range(4):
        arrive(n)
    fp[:, 2 : 2 + depth, 6:8, :] = fy_in[0]
    fp[:, 2 : 2 + depth, 8 + rows : 10 + rows, :] = fy_in[1]
    load[6].wait()
    load[7].wait()
    store_fine = pltpu.make_async_copy(fnext, fnext_hbm, store_sem.at[0])
    for z in range(depth):
        shear, first, density, metric = (fmedia[i, z] for i in range(4))
        scale = step_scale / density
        both = first + shear
        for c in range(comps):
            k = c * depth + z
            mid, along_x, along_y, along_z = stencil_xy(fp, fx_in.at[0], fx_in.at[1], c, z, k)
            along_z = metric * along_z
            along = (along_x, along_y, along_z)[c]
            accel = shear * (along_x + along_y + along_z) + both * along
            fnext[c, z] = 2.0 * mid - fprev[c, z] + scale * accel
    store_fine.start()

    for n in range(4, 8):
        arrive(n)
    cp[:, 2 : 2 + depth, 6:8, :] = cy_in[0]
    cp[:, 2 : 2 + depth, 8 + crows : 10 + crows, :] = cy_in[1]
    load[8].wait()
    load[9].wait()
    swap.wait_recv()
    own = pl.ds(pl.multiple_of(gz * crows, 8), crows)
    for c in range(comps):
        ghost[c] = partial[c, own, :] + peer_part[c]
        cp[c, 1, 8 : 8 + crows, :] = ghost[c]
    store_ghost = pltpu.make_async_copy(ghost, ghost_hbm, store_sem.at[1])
    store_ghost.start()
    for z in range(depth):
        shear, first, density = (cmedia[i, z] for i in range(3))
        scale = (step_scale / 4.0) / density
        both = first + shear
        for c in range(comps):
            k = c * depth + z
            mid, along_x, along_y, along_z = stencil_xy(cp, cx_in.at[0], cx_in.at[1], c, z, k)
            along = (along_x, along_y, along_z)[c]
            accel = shear * (along_x + along_y + along_z) + both * along
            cnext[c, z] = 2.0 * mid - cprev[c, z] + scale * accel
    store_coarse = pltpu.make_async_copy(cnext, cnext_hbm, store_sem.at[2])
    store_coarse.start()

    for n in range(8):

        @pl.when(has[n])
        def _():
            halo(n).wait_send()

    swap.wait_send()
    store_fine.wait()
    store_ghost.wait()
    store_coarse.wait()


def shards(
    sizes,
    fine_disp,
    fine_prev,
    fine_media,
    coarse_disp,
    coarse_prev,
    coarse_media,
    source_cell,
    target_cell,
    target_owner,
    target_weight,
    used_count,
):
    f32 = jnp.float32
    comps, depth, rows, cols = fine_disp.shape
    crows, ccols = coarse_disp.shape[2:]
    entries = source_cell.shape[-1]
    lists = [
        a.reshape(entries // 128, 128)
        for a in (source_cell, target_cell, target_owner, target_weight)
    ]
    entry = (entries // 128, 128)
    vm = pltpu.VMEM
    group = cols // 256 * rows
    n_gz = sizes[2]
    any_space = pl.BlockSpec(memory_space=pl.ANY)
    return pl.pallas_call(
        functools.partial(kernel, sizes),
        out_shape=(
            jax.ShapeDtypeStruct(fine_disp.shape, f32),
            jax.ShapeDtypeStruct(coarse_disp.shape, f32),
            jax.ShapeDtypeStruct((comps, crows, ccols), f32),
        ),
        in_specs=[pl.BlockSpec(memory_space=pltpu.SMEM)] + [any_space] * 10,
        out_specs=(any_space,) * 3,
        scratch_shapes=[
            vm((comps, depth + 4, rows + 16, cols), f32),
            vm(fine_prev.shape, f32),
            vm(fine_media.shape, f32),
            vm((comps, depth + 4, crows + 16, ccols), f32),
            vm(coarse_prev.shape, f32),
            vm(coarse_media.shape, f32),
            vm(entry, jnp.int32),
            vm(entry, jnp.int32),
            vm(entry, jnp.int32),
            vm(entry, f32),
            vm(fine_prev.shape, f32),
            vm(coarse_prev.shape, f32),
            vm((comps, crows, ccols), f32),
            vm((2, comps, depth, 2, cols), f32),
            vm((2, comps, depth, 2, cols), f32),
            vm((2, rows, 128), f32),
            vm((2, rows, 128), f32),
            vm((2, comps, depth, 2, ccols), f32),
            vm((2, comps, depth, 2, ccols), f32),
            vm((2, crows, 128), f32),
            vm((2, crows, 128), f32),
            vm(entry, f32),
            vm(entry, f32),
            vm(entry, f32),
            vm(entry, f32),
            vm((2 * comps * n_gz * crows, ccols), f32),
            vm((comps, n_gz * crows, ccols), f32),
            vm((comps, crows, ccols), f32),
            pltpu.SemaphoreType.DMA((10,)),
            pltpu.SemaphoreType.DMA((3,)),
            pltpu.SemaphoreType.DMA((9,)),
            pltpu.SemaphoreType.DMA((9,)),
        ],
        compiler_params=pltpu.CompilerParams(
            collective_id=0, has_side_effects=True, vmem_limit_bytes=32 * 1024 * 1024
        ),
    )(
        used_count,
        fine_disp,
        fine_prev,
        fine_media,
        coarse_disp,
        coarse_prev,
        coarse_media,
        *lists,
    )


def solution(mesh):
    sizes = (mesh.shape["gx"], mesh.shape["gy"], mesh.shape["gz"])
    fine = P(None, None, ("gy", "gz"), "gx")
    coarse = P(None, None, "gy", ("gx", "gz"))
    entry = P("gx", ("gy", "gz"), None)
    in_specs = (fine,) * 3 + (coarse,) * 3 + (entry,) * 4 + (P("gx", ("gy", "gz")),)
    out_specs = (fine, coarse, P(None, "gy", ("gx", "gz")))
    return jax.shard_map(
        functools.partial(shards, sizes),
        mesh=mesh,
        in_specs=in_specs,
        out_specs=out_specs,
        check_vma=False,
    )
```

```python
import functools

import jax
import jax.numpy as jnp
from jax import lax
from jax.experimental import pallas as pl
from jax.experimental.pallas import tpu as pltpu
from jax.sharding import PartitionSpec as P

step_scale = 0.02
MESH = pl.DeviceIdType.MESH
CHUNK_ROWS = 8
EARLY_TURNS = 1


def rows_of(ref, start, count):
    return jnp.concatenate([ref[pl.ds(start + q, 1), :] for q in range(count)], axis=1)


def second(values):
    low2, low1, mid, high1, high2 = values
    return (16.0 * (low1 + high1) - (low2 + high2) - 30.0 * mid) * (1.0 / 12.0)


def pack_columns(ref, out_ref, first, lane0, depth, comps):
    rows = out_ref.shape[0]
    lane = lax.broadcasted_iota(jnp.int32, (rows, 128), 1) // 2
    total = jnp.zeros((rows, 128), jnp.float32)
    for c in range(comps):
        for z in range(depth):
            k = c * depth + z
            tile = ref[c, 2 + z, 8 : 8 + rows, first : first + 128]
            total = jnp.where(lane == k, pltpu.roll(tile, (2 * k - lane0) % 128, 1), total)
    out_ref[...] = total


def stencil_xy(ref, from_low, from_high, c, z, k):
    rows = from_low.shape[0]
    cols = ref.shape[3]
    wide = cols + 256
    mid = ref[c, 2 + z, 8 : 8 + rows, :]
    left = pltpu.roll(from_low[...], 126 - 2 * k, 1)
    right = pltpu.roll(from_high[...], (128 - 2 * k) % 128, 1)
    ext = jnp.concatenate([left, mid, right], axis=1)
    moved = [pltpu.roll(ext, s % wide, 1)[:, 128 : 128 + cols] for s in (2, 1, -1, -2)]
    along_x = second((moved[0], moved[1], mid, moved[2], moved[3]))
    shifted = [ref[c, 2 + z, 6 + s : 6 + s + rows, :] for s in (0, 1, 3, 4)]
    along_y = second((shifted[0], shifted[1], mid, shifted[2], shifted[3]))
    along_z = second(
        (
            ref[c, z, 8 : 8 + rows, :],
            ref[c, z + 1, 8 : 8 + rows, :],
            mid,
            ref[c, z + 3, 8 : 8 + rows, :],
            ref[c, z + 4, 8 : 8 + rows, :],
        )
    )
    return mid, along_x, along_y, along_z


def kernel(
    sizes,
    count_hbm,
    fine_hbm,
    fprev_hbm,
    fmedia_hbm,
    coarse_hbm,
    cprev_hbm,
    cmedia_hbm,
    source_hbm,
    target_hbm,
    owner_hbm,
    weight_hbm,
    fnext,
    cnext,
    ghost,
    count_ref,
    fp,
    fprev,
    fmedia,
    cp,
    cprev,
    cmedia,
    source,
    target,
    owner,
    weight,
    fy_out,
    fy_in,
    fx_out,
    fx_in,
    cy_out,
    cy_in,
    cx_out,
    cx_in,
    src_lo,
    src_hi,
    tgt_lo,
    tgt_hi,
    total,
    partial,
    peer_part,
    load_sem,
    send_sem,
    recv_sem,
):
    n_gx, n_gy, n_gz = sizes
    comps, depth, rows, cols = fprev.shape
    crows, ccols = cprev.shape[2:]
    gx = lax.axis_index("gx")
    gy = lax.axis_index("gy")
    gz = lax.axis_index("gz")

    loads = [
        (fine_hbm.at[:, depth - 1 :], fp.at[:, 1 + depth : 2 + depth, 8 : 8 + rows, :]),
        (source_hbm, source),
        (target_hbm, target),
        (owner_hbm, owner),
        (weight_hbm, weight),
        (count_hbm, count_ref),
        (fine_hbm.at[:, : depth - 1], fp.at[:, 2 : 1 + depth, 8 : 8 + rows, :]),
        (coarse_hbm, cp.at[:, 2 : 2 + depth, 8 : 8 + crows, :]),
        (fmedia_hbm, fmedia),
        (fprev_hbm, fprev),
        (cmedia_hbm, cmedia),
        (cprev_hbm, cprev),
    ]
    load = [pltpu.make_async_copy(a, b, load_sem.at[i]) for i, (a, b) in enumerate(loads)]
    for copy in load:
        copy.start()

    fine_y = gy * n_gz + gz
    coarse_x = gx * n_gz + gz
    has = [
        fine_y > 0,
        fine_y < n_gy * n_gz - 1,
        gx > 0,
        gx < n_gx - 1,
        gy > 0,
        gy < n_gy - 1,
        coarse_x > 0,
        coarse_x < n_gx * n_gz - 1,
    ]
    y_low, y_high = fine_y - 1, fine_y + 1
    x_low, x_high = coarse_x - 1, coarse_x + 1
    where_to = [
        (gx, lax.div(y_low, n_gz), lax.rem(y_low, n_gz)),
        (gx, lax.div(y_high, n_gz), lax.rem(y_high, n_gz)),
        (gx - 1, gy, gz),
        (gx + 1, gy, gz),
        (gx, gy - 1, gz),
        (gx, gy + 1, gz),
        (lax.div(x_low, n_gz), gy, lax.rem(x_low, n_gz)),
        (lax.div(x_high, n_gz), gy, lax.rem(x_high, n_gz)),
    ]
    buffers = [fy_out, fy_out, fx_out, fx_out, cy_out, cy_out, cx_out, cx_out]
    landing = [fy_in, fy_in, fx_in, fx_in, cy_in, cy_in, cx_in, cx_in]
    peer = (gx, gy, n_gz - 1 - gz)

    barrier = pltpu.get_barrier_semaphore()
    expected = 1
    pl.semaphore_signal(barrier, inc=1, device_id=peer, device_id_type=MESH)
    for n in range(8):
        expected = expected + has[n].astype(jnp.int32)

        @pl.when(has[n])
        def _():
            pl.semaphore_signal(barrier, inc=1, device_id=where_to[n], device_id_type=MESH)

        @pl.when(jnp.logical_not(has[n]))
        def _():
            landing[n][n % 2] = jnp.zeros(landing[n].shape[1:], jnp.float32)

    zero_fine = jnp.zeros((comps, 2, rows, cols), jnp.float32)
    fp[:, 0:2, 8 : 8 + rows, :] = zero_fine
    fp[:, 2 + depth : 4 + depth, 8 : 8 + rows, :] = zero_fine
    zero_coarse = jnp.zeros((comps, 2, crows, ccols), jnp.float32)
    cp[:, 0:2, 8 : 8 + crows, :] = zero_coarse
    cp[:, 2 + depth : 4 + depth, 8 : 8 + crows, :] = zero_coarse

    def halo(n):
        return pltpu.make_async_remote_copy(
            src_ref=buffers[n].at[n % 2],
            dst_ref=landing[n].at[1 - n % 2],
            send_sem=send_sem.at[n],
            recv_sem=recv_sem.at[n],
            device_id=where_to[n],
            device_id_type=MESH,
        )

    load[0].wait()
    half = 256
    halves = cols // half
    pieces = []
    for c in range(comps):
        for h in range(halves):
            pieces.append(fp[c, 1 + depth, 8 : 8 + rows, h * half : (h + 1) * half])
    plane = jnp.concatenate(pieces, axis=0)
    plane_high = plane.astype(jnp.bfloat16)
    plane_low = (plane - plane_high.astype(jnp.float32)).astype(jnp.bfloat16)
    plane = jnp.concatenate([plane_high, plane_low], axis=0)
    group = halves * rows

    for i in range(1, 6):
        load[i].wait()
    cell = source[...]
    src_lo[...] = (cell % half).astype(jnp.float32)
    src_hi[...] = ((cell % cols) // half * rows + cell // cols).astype(jnp.float32)
    cell = target[...]
    tgt_lo[...] = (cell % ccols).astype(jnp.float32)
    tgt_hi[...] = (owner[...] % n_gz * crows + cell // ccols).astype(jnp.float32)
    entry_rows = source.shape[0]
    place = lax.broadcasted_iota(jnp.int32, (entry_rows, 128), 0) * 128
    place = place + lax.broadcasted_iota(jnp.int32, (entry_rows, 128), 1)
    weight[...] = jnp.where(place < count_ref[0, 0], weight[...], 0.0)

    wide = CHUNK_ROWS * 128
    base = lax.broadcasted_iota(jnp.int32, (16, wide), 0).astype(jnp.float32).astype(jnp.bfloat16)
    group_base = lax.broadcasted_iota(jnp.int32, (group, wide), 0).astype(jnp.float32)
    one = jnp.ones((16, wide), jnp.bfloat16)
    zero = jnp.zeros((16, wide), jnp.bfloat16)
    total[...] = jnp.zeros_like(total)

    def spread(row):
        return jnp.broadcast_to(row, (16, wide)).astype(jnp.bfloat16)

    def onehot(ref, start, count):
        index = spread(rows_of(ref, start, CHUNK_ROWS))
        return jnp.concatenate(
            [jnp.where(index == base + float(16 * t), one, zero) for t in range(count // 16)],
            axis=0,
        )

    def add_entries(turn):
        start = turn * CHUNK_ROWS
        picked = jnp.dot(plane, onehot(src_lo, start, half), preferred_element_type=jnp.float32)
        picked = picked[: comps * group] + picked[comps * group :]
        row_mask = jnp.broadcast_to(rows_of(src_hi, start, CHUNK_ROWS), (group, wide)) == group_base
        scale = rows_of(weight, start, CHUNK_ROWS)
        target_row = spread(rows_of(tgt_hi, start, CHUNK_ROWS))
        masks = [target_row == base + float(16 * t) for t in range(n_gz * crows // 16)]
        high_part, low_part = [], []
        for c in range(comps):
            value = jnp.where(row_mask, picked[c * group : (c + 1) * group], 0.0)
            value = jnp.sum(value, axis=0, keepdims=True) * scale
            value = jnp.broadcast_to(value, (16, wide))
            high = value.astype(jnp.bfloat16)
            low = (value - high.astype(jnp.float32)).astype(jnp.bfloat16)
            high_part += [jnp.where(mask, high, zero) for mask in masks]
            low_part += [jnp.where(mask, low, zero) for mask in masks]
        total[...] += lax.dot_general(
            jnp.concatenate(high_part + low_part, axis=0),
            onehot(tgt_lo, start, ccols),
            (((1,), (1,)), ((), ())),
            preferred_element_type=jnp.float32,
        )

    turns = entry_rows // CHUNK_ROWS
    pl.loop(0, EARLY_TURNS)(add_entries)

    load[6].wait()
    for side, first in ((0, 8), (1, 8 + rows - 2)):
        fy_out[side] = fp[:, 2 : 2 + depth, first : first + 2, :]
    pack_columns(fp, fx_out.at[0], 0, 0, depth, comps)
    pack_columns(fp, fx_out.at[1], cols - 128, 126, depth, comps)
    load[7].wait()
    for side, first in ((0, 8), (1, 8 + crows - 2)):
        cy_out[side] = cp[:, 2 : 2 + depth, first : first + 2, :]
    pack_columns(cp, cx_out.at[0], 0, 0, depth, comps)
    pack_columns(cp, cx_out.at[1], ccols - 128, 126, depth, comps)
    pl.semaphore_wait(barrier, expected)
    for n in range(8):

        @pl.when(has[n])
        def _():
            halo(n).start()

    pl.loop(EARLY_TURNS, turns)(add_entries)

    span = n_gz * crows
    for c in range(comps):
        partial[c] = (
            total[c * span : (c + 1) * span, :] + total[(comps + c) * span : (comps + c + 1) * span, :]
        )
    swap = pltpu.make_async_remote_copy(
        src_ref=partial.at[:, pl.ds(pl.multiple_of((n_gz - 1 - gz) * crows, 8), crows), :],
        dst_ref=peer_part,
        send_sem=send_sem.at[8],
        recv_sem=recv_sem.at[8],
        device_id=peer,
        device_id_type=MESH,
    )
    swap.start()

    def arrive(n):
        @pl.when(has[n ^ 1])
        def _():
            halo(n).wait_recv()

    for n in range(4):
        arrive(n)
    fp[:, 2 : 2 + depth, 6:8, :] = fy_in[0]
    fp[:, 2 : 2 + depth, 8 + rows : 10 + rows, :] = fy_in[1]
    load[8].wait()
    load[9].wait()
    for z in range(depth):
        shear, first, density, metric = (fmedia[i, z] for i in range(4))
        scale = step_scale / density
        both = first + shear
        for c in range(comps):
            k = c * depth + z
            mid, along_x, along_y, along_z = stencil_xy(fp, fx_in.at[0], fx_in.at[1], c, z, k)
            along_z = metric * along_z
            along = (along_x, along_y, along_z)[c]
            accel = shear * (along_x + along_y + along_z) + both * along
            fnext[c, z] = 2.0 * mid - fprev[c, z] + scale * accel

    for n in range(4, 8):
        arrive(n)
    cp[:, 2 : 2 + depth, 6:8, :] = cy_in[0]
    cp[:, 2 : 2 + depth, 8 + crows : 10 + crows, :] = cy_in[1]
    load[10].wait()
    load[11].wait()
    for z in range(depth):
        shear, first, density = (cmedia[i, z] for i in range(3))
        scale = (step_scale / 4.0) / density
        both = first + shear
        for c in range(comps):
            k = c * depth + z
            mid, along_x, along_y, along_z = stencil_xy(cp, cx_in.at[0], cx_in.at[1], c, z, k)
            along = (along_x, along_y, along_z)[c]
            accel = shear * (along_x + along_y + along_z) + both * along
            cnext[c, z] = 2.0 * mid - cprev[c, z] + scale * accel

    swap.wait_recv()
    own = pl.ds(pl.multiple_of(gz * crows, 8), crows)
    for c in range(comps):
        column = partial[c, own, :] + peer_part[c]
        ghost[c] = column
        for z, share in ((0, 16.0 / 12.0), (1, -1.0 / 12.0)):
            shear, first, density = (cmedia[i, z] for i in range(3))
            factor = shear + (first + shear) if c == 2 else shear
            cnext[c, z] += (share * step_scale / 4.0) / density * factor * column

    for n in range(8):

        @pl.when(has[n])
        def _():
            halo(n).wait_send()

    swap.wait_send()


def store(fnext, cnext, ghost, fnext_hbm, cnext_hbm, ghost_hbm, sem):
    pairs = ((fnext, fnext_hbm), (cnext, cnext_hbm), (ghost, ghost_hbm))
    copies = [pltpu.make_async_copy(a, b, sem.at[i]) for i, (a, b) in enumerate(pairs)]
    for copy in copies:
        copy.start()
    for copy in copies:
        copy.wait()


def shards(
    sizes,
    fine_disp,
    fine_prev,
    fine_media,
    coarse_disp,
    coarse_prev,
    coarse_media,
    source_cell,
    target_cell,
    target_owner,
    target_weight,
    used_count,
):
    f32 = jnp.float32
    comps, depth, rows, cols = fine_disp.shape
    crows, ccols = coarse_disp.shape[2:]
    entries = source_cell.shape[-1]
    lists = [
        a.reshape(entries // 128, 128)
        for a in (source_cell, target_cell, target_owner, target_weight)
    ]
    entry = (entries // 128, 128)
    vm = pltpu.VMEM
    group = cols // 256 * rows
    n_gz = sizes[2]
    in_hbm = pl.BlockSpec(memory_space=pltpu.HBM)
    out_shape = (
        jax.ShapeDtypeStruct(fine_disp.shape, f32),
        jax.ShapeDtypeStruct(coarse_disp.shape, f32),
        jax.ShapeDtypeStruct((comps, crows, ccols), f32),
    )
    results = pl.pallas_call(
        functools.partial(kernel, sizes),
        out_shape=tuple(vm(o.shape, o.dtype) for o in out_shape),
        in_specs=[in_hbm] * 11,
        out_specs=(pl.BlockSpec(memory_space=pltpu.VMEM),) * 3,
        scratch_shapes=[
            pltpu.SMEM((1, 1), jnp.int32),
            vm((comps, depth + 4, rows + 16, cols), f32),
            vm(fine_prev.shape, f32),
            vm(fine_media.shape, f32),
            vm((comps, depth + 4, crows + 16, ccols), f32),
            vm(coarse_prev.shape, f32),
            vm(coarse_media.shape, f32),
            vm(entry, jnp.int32),
            vm(entry, jnp.int32),
            vm(entry, jnp.int32),
            vm(entry, f32),
            vm((2, comps, depth, 2, cols), f32),
            vm((2, comps, depth, 2, cols), f32),
            vm((2, rows, 128), f32),
            vm((2, rows, 128), f32),
            vm((2, comps, depth, 2, ccols), f32),
            vm((2, comps, depth, 2, ccols), f32),
            vm((2, crows, 128), f32),
            vm((2, crows, 128), f32),
            vm(entry, f32),
            vm(entry, f32),
            vm(entry, f32),
            vm(entry, f32),
            vm((2 * comps * n_gz * crows, ccols), f32),
            vm((comps, n_gz * crows, ccols), f32),
            vm((comps, crows, ccols), f32),
            pltpu.SemaphoreType.DMA((12,)),
            pltpu.SemaphoreType.DMA((9,)),
            pltpu.SemaphoreType.DMA((9,)),
        ],
        compiler_params=pltpu.CompilerParams(
            collective_id=0, has_side_effects=True, vmem_limit_bytes=32 * 1024 * 1024
        ),
    )(
        used_count,
        *(pltpu.with_memory_space_constraint(a, pltpu.HBM) for a in (fine_disp,
        fine_prev,
        fine_media,
        coarse_disp,
        coarse_prev,
        coarse_media,
        *lists)),
    )
    return pl.pallas_call(
        store,
        out_shape=out_shape,
        in_specs=[pl.BlockSpec(memory_space=pltpu.VMEM)] * 3,
        out_specs=(in_hbm,) * 3,
        scratch_shapes=[pltpu.SemaphoreType.DMA((3,))],
    )(*(pltpu.with_memory_space_constraint(a, pltpu.VMEM) for a in results))


def solution(mesh):
    sizes = (mesh.shape["gx"], mesh.shape["gy"], mesh.shape["gz"])
    fine = P(None, None, ("gy", "gz"), "gx")
    coarse = P(None, None, "gy", ("gx", "gz"))
    entry = P("gx", ("gy", "gz"), None)
    in_specs = (fine,) * 3 + (coarse,) * 3 + (entry,) * 4 + (P("gx", ("gy", "gz")),)
    out_specs = (fine, coarse, P(None, "gy", ("gx", "gz")))
    return jax.shard_map(
        functools.partial(shards, sizes),
        mesh=mesh,
        in_specs=in_specs,
        out_specs=out_specs,
        check_vma=False,
    )
```

```python
import functools

import jax
import jax.numpy as jnp
from jax import lax
from jax.experimental import pallas as pl
from jax.experimental.pallas import tpu as pltpu
from jax.sharding import PartitionSpec as P

step_scale = 0.02
MESH = pl.DeviceIdType.MESH
CHUNK_ROWS = 8
EARLY_TURNS = 1


def rows_of(ref, start, count):
    return jnp.concatenate([ref[pl.ds(start + q, 1), :] for q in range(count)], axis=1)


def second(values):
    low2, low1, mid, high1, high2 = values
    return (16.0 * (low1 + high1) - (low2 + high2) - 30.0 * mid) * (1.0 / 12.0)


def pack_columns(ref, out_ref, first, lane0, depth, comps):
    rows = out_ref.shape[0]
    lane = lax.broadcasted_iota(jnp.int32, (rows, 128), 1) // 2
    total = jnp.zeros((rows, 128), jnp.float32)
    for c in range(comps):
        for z in range(depth):
            k = c * depth + z
            tile = ref[c, 2 + z, 8 : 8 + rows, first : first + 128]
            total = jnp.where(lane == k, pltpu.roll(tile, (2 * k - lane0) % 128, 1), total)
    out_ref[...] = total


def stencil_xy(ref, rows, c, z):
    cols = ref.shape[3]
    wide = cols + 256
    mid = ref[c, 2 + z, 8 : 8 + rows, :]
    edge = jnp.zeros((rows, 128), jnp.float32)
    ext = jnp.concatenate([edge, mid, edge], axis=1)
    moved = [pltpu.roll(ext, s % wide, 1)[:, 128 : 128 + cols] for s in (2, 1, -1, -2)]
    along_x = second((moved[0], moved[1], mid, moved[2], moved[3]))
    shifted = [ref[c, 2 + z, 6 + s : 6 + s + rows, :] for s in (0, 1, 3, 4)]
    along_y = second((shifted[0], shifted[1], mid, shifted[2], shifted[3]))
    along_z = second(
        (
            ref[c, z, 8 : 8 + rows, :],
            ref[c, z + 1, 8 : 8 + rows, :],
            mid,
            ref[c, z + 3, 8 : 8 + rows, :],
            ref[c, z + 4, 8 : 8 + rows, :],
        )
    )
    return mid, along_x, along_y, along_z


def add_halos(out, media, y_in, x_in, step):
    comps, depth, rows, cols = out.shape
    row = lax.broadcasted_iota(jnp.int32, (8, cols), 0)
    lane = lax.broadcasted_iota(jnp.int32, (rows, 128), 1)
    twelfth = 1.0 / 12.0
    for z in range(depth):
        shear, first, density = (media[i, z] for i in range(3))
        scale = step / density
        plain = scale * shear
        full = plain + scale * (first + shear)
        for c in range(comps):
            k = c * depth + z
            factor = full if c == 1 else plain
            outer, inner = y_in[0, c, z, 0:1, :], y_in[0, c, z, 1:2, :]
            low = jnp.where(row == 1, -twelfth * inner, 0.0)
            low = jnp.where(row == 0, (16.0 * inner - outer) * twelfth, low)
            inner, outer = y_in[1, c, z, 0:1, :], y_in[1, c, z, 1:2, :]
            high = jnp.where(row == 6, -twelfth * inner, 0.0)
            high = jnp.where(row == 7, (16.0 * inner - outer) * twelfth, high)
            out[c, z, 0:8, :] += factor[0:8] * low
            out[c, z, rows - 8 : rows, :] += factor[rows - 8 : rows] * high
            factor = full if c == 0 else plain
            near = pltpu.roll(x_in[0], (127 - 2 * k) % 128, 1)
            both = pltpu.roll(x_in[0], (128 - 2 * k) % 128, 1)
            low = jnp.where(lane == 1, -twelfth * both, 0.0)
            low = jnp.where(lane == 0, (16.0 * near - both) * twelfth, low)
            near = pltpu.roll(x_in[1], (127 - 2 * k) % 128, 1)
            both = pltpu.roll(x_in[1], (126 - 2 * k) % 128, 1)
            high = jnp.where(lane == 126, -twelfth * both, 0.0)
            high = jnp.where(lane == 127, (16.0 * near - both) * twelfth, high)
            out[c, z, :, 0:128] += factor[:, 0:128] * low
            out[c, z, :, cols - 128 : cols] += factor[:, cols - 128 : cols] * high


def kernel(
    sizes,
    count_hbm,
    fine_hbm,
    fprev_hbm,
    fmedia_hbm,
    coarse_hbm,
    cprev_hbm,
    cmedia_hbm,
    source_hbm,
    target_hbm,
    owner_hbm,
    weight_hbm,
    fnext,
    cnext,
    ghost,
    count_ref,
    fp,
    fprev,
    fmedia,
    cp,
    cprev,
    cmedia,
    source,
    target,
    owner,
    weight,
    fy_out,
    fy_in,
    fx_out,
    fx_in,
    cy_out,
    cy_in,
    cx_out,
    cx_in,
    src_lo,
    src_hi,
    tgt_lo,
    tgt_hi,
    total,
    partial,
    peer_part,
    load_sem,
    send_sem,
    recv_sem,
):
    n_gx, n_gy, n_gz = sizes
    comps, depth, rows, cols = fprev.shape
    crows, ccols = cprev.shape[2:]
    gx = lax.axis_index("gx")
    gy = lax.axis_index("gy")
    gz = lax.axis_index("gz")

    loads = [
        (fine_hbm.at[:, depth - 1 :], fp.at[:, 1 + depth : 2 + depth, 8 : 8 + rows, :]),
        (source_hbm, source),
        (target_hbm, target),
        (owner_hbm, owner),
        (weight_hbm, weight),
        (count_hbm, count_ref),
        (fine_hbm.at[:, : depth - 1], fp.at[:, 2 : 1 + depth, 8 : 8 + rows, :]),
        (coarse_hbm, cp.at[:, 2 : 2 + depth, 8 : 8 + crows, :]),
        (fmedia_hbm, fmedia),
        (fprev_hbm, fprev),
        (cmedia_hbm, cmedia),
        (cprev_hbm, cprev),
    ]
    load = [pltpu.make_async_copy(a, b, load_sem.at[i]) for i, (a, b) in enumerate(loads)]
    for copy in load:
        copy.start()

    fine_y = gy * n_gz + gz
    coarse_x = gx * n_gz + gz
    has = [
        fine_y > 0,
        fine_y < n_gy * n_gz - 1,
        gx > 0,
        gx < n_gx - 1,
        gy > 0,
        gy < n_gy - 1,
        coarse_x > 0,
        coarse_x < n_gx * n_gz - 1,
    ]
    y_low, y_high = fine_y - 1, fine_y + 1
    x_low, x_high = coarse_x - 1, coarse_x + 1
    where_to = [
        (gx, lax.div(y_low, n_gz), lax.rem(y_low, n_gz)),
        (gx, lax.div(y_high, n_gz), lax.rem(y_high, n_gz)),
        (gx - 1, gy, gz),
        (gx + 1, gy, gz),
        (gx, gy - 1, gz),
        (gx, gy + 1, gz),
        (lax.div(x_low, n_gz), gy, lax.rem(x_low, n_gz)),
        (lax.div(x_high, n_gz), gy, lax.rem(x_high, n_gz)),
    ]
    buffers = [fy_out, fy_out, fx_out, fx_out, cy_out, cy_out, cx_out, cx_out]
    landing = [fy_in, fy_in, fx_in, fx_in, cy_in, cy_in, cx_in, cx_in]
    peer = (gx, gy, n_gz - 1 - gz)

    barrier = pltpu.get_barrier_semaphore()
    expected = 1
    pl.semaphore_signal(barrier, inc=1, device_id=peer, device_id_type=MESH)
    for n in range(8):
        expected = expected + has[n].astype(jnp.int32)

        @pl.when(has[n])
        def _():
            pl.semaphore_signal(barrier, inc=1, device_id=where_to[n], device_id_type=MESH)

        @pl.when(jnp.logical_not(has[n]))
        def _():
            landing[n][n % 2] = jnp.zeros(landing[n].shape[1:], jnp.float32)

    zero_fine = jnp.zeros((comps, 2, rows, cols), jnp.float32)
    fp[:, 0:2, 8 : 8 + rows, :] = zero_fine
    fp[:, 2 + depth : 4 + depth, 8 : 8 + rows, :] = zero_fine
    zero_coarse = jnp.zeros((comps, 2, crows, ccols), jnp.float32)
    cp[:, 0:2, 8 : 8 + crows, :] = zero_coarse
    cp[:, 2 + depth : 4 + depth, 8 : 8 + crows, :] = zero_coarse

    def halo(n):
        return pltpu.make_async_remote_copy(
            src_ref=buffers[n].at[n % 2],
            dst_ref=landing[n].at[1 - n % 2],
            send_sem=send_sem.at[n],
            recv_sem=recv_sem.at[n],
            device_id=where_to[n],
            device_id_type=MESH,
        )

    load[0].wait()
    half = 256
    halves = cols // half
    pieces = []
    for c in range(comps):
        for h in range(halves):
            pieces.append(fp[c, 1 + depth, 8 : 8 + rows, h * half : (h + 1) * half])
    plane = jnp.concatenate(pieces, axis=0)
    plane_high = plane.astype(jnp.bfloat16)
    plane_low = (plane - plane_high.astype(jnp.float32)).astype(jnp.bfloat16)
    plane = jnp.concatenate([plane_high, plane_low], axis=0)
    group = halves * rows

    for i in range(1, 6):
        load[i].wait()
    cell = source[...]
    src_lo[...] = (cell % half).astype(jnp.float32)
    src_hi[...] = ((cell % cols) // half * rows + cell // cols).astype(jnp.float32)
    cell = target[...]
    tgt_lo[...] = (cell % ccols).astype(jnp.float32)
    tgt_hi[...] = (owner[...] % n_gz * crows + cell // ccols).astype(jnp.float32)
    entry_rows = source.shape[0]
    place = lax.broadcasted_iota(jnp.int32, (entry_rows, 128), 0) * 128
    place = place + lax.broadcasted_iota(jnp.int32, (entry_rows, 128), 1)
    weight[...] = jnp.where(place < count_ref[0, 0], weight[...], 0.0)

    wide = CHUNK_ROWS * 128
    base = lax.broadcasted_iota(jnp.int32, (16, wide), 0).astype(jnp.float32).astype(jnp.bfloat16)
    group_base = lax.broadcasted_iota(jnp.int32, (group, wide), 0).astype(jnp.float32)
    one = jnp.ones((16, wide), jnp.bfloat16)
    zero = jnp.zeros((16, wide), jnp.bfloat16)
    total[...] = jnp.zeros_like(total)

    def spread(row):
        return jnp.broadcast_to(row, (16, wide)).astype(jnp.bfloat16)

    def onehot(ref, start, count):
        index = spread(rows_of(ref, start, CHUNK_ROWS))
        return jnp.concatenate(
            [jnp.where(index == base + float(16 * t), one, zero) for t in range(count // 16)],
            axis=0,
        )

    def add_entries(turn):
        start = turn * CHUNK_ROWS
        picked = jnp.dot(plane, onehot(src_lo, start, half), preferred_element_type=jnp.float32)
        picked = picked[: comps * group] + picked[comps * group :]
        row_mask = jnp.broadcast_to(rows_of(src_hi, start, CHUNK_ROWS), (group, wide)) == group_base
        scale = rows_of(weight, start, CHUNK_ROWS)
        target_row = spread(rows_of(tgt_hi, start, CHUNK_ROWS))
        masks = [target_row == base + float(16 * t) for t in range(n_gz * crows // 16)]
        high_part, low_part = [], []
        for c in range(comps):
            value = jnp.where(row_mask, picked[c * group : (c + 1) * group], 0.0)
            value = jnp.sum(value, axis=0, keepdims=True) * scale
            value = jnp.broadcast_to(value, (16, wide))
            high = value.astype(jnp.bfloat16)
            low = (value - high.astype(jnp.float32)).astype(jnp.bfloat16)
            high_part += [jnp.where(mask, high, zero) for mask in masks]
            low_part += [jnp.where(mask, low, zero) for mask in masks]
        total[...] += lax.dot_general(
            jnp.concatenate(high_part + low_part, axis=0),
            onehot(tgt_lo, start, ccols),
            (((1,), (1,)), ((), ())),
            preferred_element_type=jnp.float32,
        )

    turns = entry_rows // CHUNK_ROWS
    pl.loop(0, EARLY_TURNS)(add_entries)

    load[6].wait()
    for side, first in ((0, 8), (1, 8 + rows - 2)):
        fy_out[side] = fp[:, 2 : 2 + depth, first : first + 2, :]
    pack_columns(fp, fx_out.at[0], 0, 0, depth, comps)
    pack_columns(fp, fx_out.at[1], cols - 128, 126, depth, comps)
    load[7].wait()
    for side, first in ((0, 8), (1, 8 + crows - 2)):
        cy_out[side] = cp[:, 2 : 2 + depth, first : first + 2, :]
    pack_columns(cp, cx_out.at[0], 0, 0, depth, comps)
    pack_columns(cp, cx_out.at[1], ccols - 128, 126, depth, comps)
    pl.semaphore_wait(barrier, expected)
    for n in range(8):

        @pl.when(has[n])
        def _():
            halo(n).start()

    pl.loop(EARLY_TURNS, turns)(add_entries)

    span = n_gz * crows
    for c in range(comps):
        partial[c] = (
            total[c * span : (c + 1) * span, :] + total[(comps + c) * span : (comps + c + 1) * span, :]
        )
    swap = pltpu.make_async_remote_copy(
        src_ref=partial.at[:, pl.ds(pl.multiple_of((n_gz - 1 - gz) * crows, 8), crows), :],
        dst_ref=peer_part,
        send_sem=send_sem.at[8],
        recv_sem=recv_sem.at[8],
        device_id=peer,
        device_id_type=MESH,
    )
    swap.start()

    def arrive(n):
        @pl.when(has[n ^ 1])
        def _():
            halo(n).wait_recv()

    edge_rows = jnp.zeros((comps, depth, 2, cols), jnp.float32)
    fp[:, 2 : 2 + depth, 6:8, :] = edge_rows
    fp[:, 2 : 2 + depth, 8 + rows : 10 + rows, :] = edge_rows
    load[8].wait()
    load[9].wait()
    for z in range(depth):
        shear, first, density, metric = (fmedia[i, z] for i in range(4))
        scale = step_scale / density
        both = first + shear
        for c in range(comps):
            mid, along_x, along_y, along_z = stencil_xy(fp, rows, c, z)
            along_z = metric * along_z
            along = (along_x, along_y, along_z)[c]
            accel = shear * (along_x + along_y + along_z) + both * along
            fnext[c, z] = 2.0 * mid - fprev[c, z] + scale * accel

    edge_rows = jnp.zeros((comps, depth, 2, ccols), jnp.float32)
    cp[:, 2 : 2 + depth, 6:8, :] = edge_rows
    cp[:, 2 : 2 + depth, 8 + crows : 10 + crows, :] = edge_rows
    load[10].wait()
    load[11].wait()
    for z in range(depth):
        shear, first, density = (cmedia[i, z] for i in range(3))
        scale = (step_scale / 4.0) / density
        both = first + shear
        for c in range(comps):
            mid, along_x, along_y, along_z = stencil_xy(cp, crows, c, z)
            along = (along_x, along_y, along_z)[c]
            accel = shear * (along_x + along_y + along_z) + both * along
            cnext[c, z] = 2.0 * mid - cprev[c, z] + scale * accel

    for n in range(8):
        arrive(n)
    add_halos(fnext, fmedia, fy_in, fx_in, step_scale)
    add_halos(cnext, cmedia, cy_in, cx_in, step_scale / 4.0)

    swap.wait_recv()
    own = pl.ds(pl.multiple_of(gz * crows, 8), crows)
    for c in range(comps):
        column = partial[c, own, :] + peer_part[c]
        ghost[c] = column
        for z, share in ((0, 16.0 / 12.0), (1, -1.0 / 12.0)):
            shear, first, density = (cmedia[i, z] for i in range(3))
            factor = shear + (first + shear) if c == 2 else shear
            cnext[c, z] += (share * step_scale / 4.0) / density * factor * column

    for n in range(8):

        @pl.when(has[n])
        def _():
            halo(n).wait_send()

    swap.wait_send()


def store(fnext, cnext, ghost, fnext_hbm, cnext_hbm, ghost_hbm, sem):
    pairs = ((fnext, fnext_hbm), (cnext, cnext_hbm), (ghost, ghost_hbm))
    copies = [pltpu.make_async_copy(a, b, sem.at[i]) for i, (a, b) in enumerate(pairs)]
    for copy in copies:
        copy.start()
    for copy in copies:
        copy.wait()


def shards(
    sizes,
    fine_disp,
    fine_prev,
    fine_media,
    coarse_disp,
    coarse_prev,
    coarse_media,
    source_cell,
    target_cell,
    target_owner,
    target_weight,
    used_count,
):
    f32 = jnp.float32
    comps, depth, rows, cols = fine_disp.shape
    crows, ccols = coarse_disp.shape[2:]
    entries = source_cell.shape[-1]
    lists = [
        a.reshape(entries // 128, 128)
        for a in (source_cell, target_cell, target_owner, target_weight)
    ]
    entry = (entries // 128, 128)
    vm = pltpu.VMEM
    group = cols // 256 * rows
    n_gz = sizes[2]
    in_hbm = pl.BlockSpec(memory_space=pltpu.HBM)
    out_shape = (
        jax.ShapeDtypeStruct(fine_disp.shape, f32),
        jax.ShapeDtypeStruct(coarse_disp.shape, f32),
        jax.ShapeDtypeStruct((comps, crows, ccols), f32),
    )
    results = pl.pallas_call(
        functools.partial(kernel, sizes),
        out_shape=tuple(vm(o.shape, o.dtype) for o in out_shape),
        in_specs=[in_hbm] * 11,
        out_specs=(pl.BlockSpec(memory_space=pltpu.VMEM),) * 3,
        scratch_shapes=[
            pltpu.SMEM((1, 1), jnp.int32),
            vm((comps, depth + 4, rows + 16, cols), f32),
            vm(fine_prev.shape, f32),
            vm(fine_media.shape, f32),
            vm((comps, depth + 4, crows + 16, ccols), f32),
            vm(coarse_prev.shape, f32),
            vm(coarse_media.shape, f32),
            vm(entry, jnp.int32),
            vm(entry, jnp.int32),
            vm(entry, jnp.int32),
            vm(entry, f32),
            vm((2, comps, depth, 2, cols), f32),
            vm((2, comps, depth, 2, cols), f32),
            vm((2, rows, 128), f32),
            vm((2, rows, 128), f32),
            vm((2, comps, depth, 2, ccols), f32),
            vm((2, comps, depth, 2, ccols), f32),
            vm((2, crows, 128), f32),
            vm((2, crows, 128), f32),
            vm(entry, f32),
            vm(entry, f32),
            vm(entry, f32),
            vm(entry, f32),
            vm((2 * comps * n_gz * crows, ccols), f32),
            vm((comps, n_gz * crows, ccols), f32),
            vm((comps, crows, ccols), f32),
            pltpu.SemaphoreType.DMA((12,)),
            pltpu.SemaphoreType.DMA((9,)),
            pltpu.SemaphoreType.DMA((9,)),
        ],
        compiler_params=pltpu.CompilerParams(
            collective_id=0, has_side_effects=True, vmem_limit_bytes=32 * 1024 * 1024
        ),
    )(
        used_count,
        *(pltpu.with_memory_space_constraint(a, pltpu.HBM) for a in (fine_disp,
        fine_prev,
        fine_media,
        coarse_disp,
        coarse_prev,
        coarse_media,
        *lists)),
    )
    return pl.pallas_call(
        store,
        out_shape=out_shape,
        in_specs=[pl.BlockSpec(memory_space=pltpu.VMEM)] * 3,
        out_specs=(in_hbm,) * 3,
        scratch_shapes=[pltpu.SemaphoreType.DMA((3,))],
    )(*(pltpu.with_memory_space_constraint(a, pltpu.VMEM) for a in results))


def solution(mesh):
    sizes = (mesh.shape["gx"], mesh.shape["gy"], mesh.shape["gz"])
    fine = P(None, None, ("gy", "gz"), "gx")
    coarse = P(None, None, "gy", ("gx", "gz"))
    entry = P("gx", ("gy", "gz"), None)
    in_specs = (fine,) * 3 + (coarse,) * 3 + (entry,) * 4 + (P("gx", ("gy", "gz")),)
    out_specs = (fine, coarse, P(None, "gy", ("gx", "gz")))
    return jax.shard_map(
        functools.partial(shards, sizes),
        mesh=mesh,
        in_specs=in_specs,
        out_specs=out_specs,
        check_vma=False,
    )
```
